256 devices in a mesh: dp: 32 (over x, y, core), fsdp: 8 (over z).
Axes of the slice: x: 4, y: 4, z: 8, core: 2. Of those that a mesh axis runs over, the one named last changes fastest.
Arguments:
- frames: bfloat16 [131072, 1536], P(('dp', 'fsdp')), may hold values from -6 to 6
- segments: int32 [131072], replicated, may hold values from 0 to 383, never falling along the last dimension, each value on 1 to 750 neighbouring positions
- norm_gain: float32 [1536], replicated, may hold values from 0.1 to 1.9
- norm_bias: float32 [1536], replicated, may hold values from -3 to 3
- expand_weight: bfloat16 [1536, 3072], P('fsdp', 'dp'), may hold values from -0.15625 to 0.15625
- conv_kernel: float32 [31, 1536], replicated, may hold values from -1 to 1
- batch_scale: float32 [1536], replicated, may hold values from 0.1 to 1.9
- batch_shift: float32 [1536], replicated, may hold values from -3 to 3
- project_weight: bfloat16 [1536, 1536], P('fsdp', 'dp'), may hold values from -0.15625 to 0.15625
Outputs:
- output: bfloat16 [131072, 1536], P(('dp', 'fsdp'))
The draws below stay inside these ranges and needn't reach their ends.
Inputs may be any that keep to these rules, and one draw needn't show every extreme that they name: `segments`: utterance numbers never fall along the frames; each utterance is 1 to 750 frames, and one has exactly 750.
All inputs are finite; a program needn't handle non-finite values.
Results may differ from the reference program's by a relative error of at most 0.0041.
Values may be sent and summed in bfloat16 or wider, within the bound.
A program may use at most 64 MiB of HBM per device.

```python
import math
import jax
import jax.numpy as jnp
import numpy as np
from jax import lax

D = 1536
KERNEL = 31
TOK_DEV = 512
TOKENS = 131072
MOST_LEN = 750
UTTS = 384


def level_of(own_key, dims, split, smallest, largest):
    def one(dim, blocks):
        draws = jax.random.uniform(jax.random.fold_in(jax.random.fold_in(own_key, 6), dim), (blocks,), jnp.float32, smallest / len(split), largest / len(split))
        return jnp.repeat(jnp.exp(draws), dims[dim] // blocks).reshape((-1,) + (1,) * (len(dims) - dim - 1))

    factor_of = one(*split[0])
    for cut in split[1:]:
        factor_of = factor_of * one(*cut)
    return factor_of


def profile(amount, total, reach, lean):
    portions = [(1 << 20) // math.isqrt(grade ** lean) + 1 for grade in range(2, amount + 1)]
    spare, given = total - reach - (amount - 1), [1] * (amount - 1)
    while spare > 0:
        free = [i for i in range(amount - 1) if given[i] < reach]
        pool, budget = sum([portions[i] for i in free]), spare
        for i in free:
            addition = min(reach - given[i], max(1, budget * portions[i] // pool), spare)
            given[i] = given[i] + addition
            spare = spare - addition
    return np.array([reach] + given)


def ragged_sizes(stream_key, amount, total, limit, lean):
    if amount == 2:
        one = jax.random.randint(stream_key, (), max(1, total - limit), min(limit, total - 1) + 1)
        return jnp.stack([one, total - one])
    sizes = jnp.asarray(profile(amount, total, limit, lean), jnp.int32)
    couples = (amount - 1) // 2
    giver, sink = sizes[1:1 + 2 * couples:2], sizes[2:2 + 2 * couples:2]
    margin = jnp.minimum(giver - 1, limit - sink)
    passed = jax.random.randint(jax.random.fold_in(stream_key, 1), (couples,), 0, 1 << 20) % (margin + 1)
    sizes = sizes.at[1:1 + 2 * couples:2].set(giver - passed).at[2:2 + 2 * couples:2].set(sink + passed)
    return sizes[jax.random.permutation(jax.random.fold_in(stream_key, 2), amount)]


def bell_draw(own_key, extent, spread, reach, pieces=(), held_as=jnp.bfloat16):
    array = jax.random.normal(own_key, extent, jnp.float32) * spread
    if len(pieces) > 0:
        array = level_of(own_key, extent, pieces, -0.22, 0.18) * array
    return jnp.clip(array, min=-reach, max=reach).astype(held_as)


def setup_inputs(seed: int = 0) -> dict:
    seeds = jax.random.split(jax.random.key(seed), 10)
    frames = bell_draw(seeds[0], (TOKENS, D), 1.0, 6.0, ((0, 256),))
    segments = jnp.searchsorted(jnp.cumsum(ragged_sizes(seeds[1], UTTS, TOKENS, MOST_LEN, 1)), jnp.arange(TOKENS), side="right").astype(jnp.int32)
    norm_gain = jnp.clip(1.0 + 0.18 * jax.random.normal(seeds[2], (D,), jnp.float32), 0.1, 1.9)
    norm_bias = bell_draw(seeds[3], (D,), 0.5, 3.0, (), jnp.float32)
    expand_weight = bell_draw(seeds[4], (D, 2 * D), D ** -0.5, 0.15625, ((0, 8), (1, 32)))
    conv_kernel = bell_draw(seeds[5], (KERNEL, D), KERNEL ** -0.5, 1.0, (), jnp.float32)
    batch_scale = jnp.clip(1.0 + 0.18 * jax.random.normal(seeds[6], (D,), jnp.float32), 0.1, 1.9)
    batch_shift = bell_draw(seeds[7], (D,), 0.5, 3.0, (), jnp.float32)
    project_weight = bell_draw(seeds[8], (D, D), D ** -0.5, 0.15625, ((0, 8), (1, 32)))
    return dict(frames=frames, segments=segments, norm_gain=norm_gain, norm_bias=norm_bias, expand_weight=expand_weight, conv_kernel=conv_kernel, batch_scale=batch_scale, batch_shift=batch_shift, project_weight=project_weight)


EPSILON = 1e-05

def layer_norm(source, norm_gain, norm_bias):
    values = source.astype(jnp.float32)
    average = lax.optimization_barrier(jnp.mean(values, axis=-1, keepdims=True))
    centered = values - average
    variance = lax.optimization_barrier(jnp.mean(centered * centered, axis=-1, keepdims=True))
    return (centered * lax.rsqrt(variance + EPSILON) * norm_gain + norm_bias).astype(jnp.bfloat16)

def gated_units(expanded):
    channels = expanded.shape[1] // 2
    return (expanded[:, :channels] * jax.nn.sigmoid(expanded[:, channels:])).astype(jnp.bfloat16)

def depthwise(gated_ext, segment_ext, conv_kernel, row_count):
    half_span = conv_kernel.shape[0] // 2
    center = segment_ext[half_span:half_span + row_count]
    summed = jnp.zeros((row_count, gated_ext.shape[1]), jnp.float32)
    for offset in range(conv_kernel.shape[0]):
        same_utterance = (segment_ext[offset:offset + row_count] == center).astype(jnp.float32)
        shifted = gated_ext[offset:offset + row_count].astype(jnp.float32)
        summed = summed + conv_kernel[offset] * (shifted * same_utterance[:, None])
    return summed

def finish(summed, batch_scale, batch_shift):
    hidden = summed * batch_scale + batch_shift
    return (hidden * jax.nn.sigmoid(hidden)).astype(jnp.bfloat16)

def reference(frames, segments, norm_gain, norm_bias, expand_weight, conv_kernel, batch_scale, batch_shift, project_weight):
    block_count = TOKENS // TOK_DEV
    half_span = KERNEL // 2
    blocked = frames.reshape(block_count, TOK_DEV, D)

    def first_pass(block_frames):
        normed = layer_norm(block_frames, norm_gain, norm_bias)
        expanded = jnp.dot(normed, expand_weight, preferred_element_type=jnp.float32)
        return gated_units(expanded)
    gated = lax.map(first_pass, blocked).reshape(TOKENS, D)
    gated_pad = jnp.pad(gated, ((half_span, half_span), (0, 0)))
    segment_pad = jnp.pad(segments, (half_span, half_span), constant_values=-1)

    def second_pass(block_number):
        first_row = (block_number * TOK_DEV).astype(jnp.int32)
        gated_ext = lax.dynamic_slice_in_dim(gated_pad, first_row, TOK_DEV + 2 * half_span, 0)
        segment_ext = lax.dynamic_slice_in_dim(segment_pad, first_row, TOK_DEV + 2 * half_span, 0)
        summed = depthwise(gated_ext, segment_ext, conv_kernel, TOK_DEV)
        activated = finish(summed, batch_scale, batch_shift)
        block_frames = lax.dynamic_slice_in_dim(frames, first_row, TOK_DEV, 0)
        product = jnp.dot(activated, project_weight, preferred_element_type=jnp.float32)
        return (product + block_frames.astype(jnp.float32)).astype(jnp.bfloat16)
    result = lax.map(second_pass, jnp.arange(block_count, dtype=jnp.int32))
    return result.reshape(TOKENS, D)
```

```python
import functools

import jax
import jax.numpy as jnp
from jax import lax
from jax.experimental import pallas as pl
from jax.experimental.pallas import tpu as pltpu
from jax.sharding import PartitionSpec as P

EPSILON = 1e-05
MESH = pl.DeviceIdType.MESH
F32 = jnp.float32
BF16 = jnp.bfloat16

NX, NY, NZ = 4, 4, 8
ROWS = 512
EDGE = 16
ALL = ROWS + 2 * EDGE
D = 1536
HALF = 15
TAPS = 31
SEMS = 256


def sigmoid(v):
    return 0.5 * jnp.tanh(0.5 * v) + 0.5


def kernel(
    frames, segs, gain, bias, w1, taps, scale, shift, w2, out,
    weights, rows, normed, active, result, gated, seg_raw, seg_col, before, after,
    own1, own2, own2r, parts1, parts2, gain_v, bias_v, taps_v, scale_v, shift_v,
    local_sem, send_sem, recv_sem,
):
    dp = lax.axis_index("dp")
    z = lax.axis_index("fsdp")
    x = dp // 8
    y = (dp // 2) % 4
    c = dp % 2
    s = 1 - 2 * c
    block = dp * 8 + z

    def dev(px, py, pz, pc):
        return (px * 8 + py * 2 + pc, pz)

    def xo(k):
        return (x + k + 2 * NX) % NX

    def yo(k):
        return (y + k + 2 * NY) % NY

    def zo(k):
        return (z + k + 2 * NZ) % NZ

    nxt = (block + 1) % 256
    prv = (block + 255) % 256
    next_dev = (nxt // 8, nxt % 8)
    prev_dev = (prv // 8, prv % 8)
    sibling = dev(x, y, z, 1 - c)
    x_dev = dev(xo(s), y, z, c)
    y_dev = dev(x, yo(s), z, c)
    z_dev = dev(x, y, zo(s), c)

    tile0 = block // 2
    seg_tiles = [
        jnp.maximum(tile0 - 1, 0),
        tile0,
        jnp.minimum(tile0 + 1, 127),
    ]
    loads = [
        pltpu.make_async_copy(w1, own1, local_sem.at[0]),
        pltpu.make_async_copy(w2, own2, local_sem.at[1]),
        pltpu.make_async_copy(frames, rows.at[pl.ds(EDGE, ROWS)], local_sem.at[2]),
        pltpu.make_async_copy(gain, gain_v, local_sem.at[3]),
        pltpu.make_async_copy(bias, bias_v, local_sem.at[4]),
        pltpu.make_async_copy(taps, taps_v, local_sem.at[5]),
        pltpu.make_async_copy(scale, scale_v, local_sem.at[6]),
        pltpu.make_async_copy(shift, shift_v, local_sem.at[7]),
    ] + [
        pltpu.make_async_copy(
            segs.at[pl.ds(pl.multiple_of(t * 8, 8), 8)],
            seg_raw.at[pl.ds(8 * i, 8)],
            local_sem.at[8 + i],
        )
        for i, t in enumerate(seg_tiles)
    ]
    for load in loads:
        load.start()

    barrier = pltpu.get_barrier_semaphore()
    peers = [
        dev(x, yo(dy), z, (c + dc) % 2) for dy in range(NY) for dc in range(2) if dy + dc
    ]
    peers += [dev(x, y, zo(k), c) for k in range(1, NZ)]
    peers += [dev(xo(k), y, z, c) for k in range(1, NX)]
    peers += [next_dev, prev_dev]
    for peer in peers:
        pl.semaphore_signal(barrier, inc=1, device_id=peer, device_id_type=MESH)
    pl.semaphore_wait(barrier, len(peers))

    count = [0]
    sent = []

    def post(src, dst, device, when=None):
        i = count[0]
        count[0] += 1
        copy = pltpu.make_async_remote_copy(
            src_ref=src, dst_ref=dst, send_sem=send_sem.at[i], recv_sem=recv_sem.at[i],
            device_id=device, device_id_type=MESH,
        )
        if when is None:
            copy.start()
            sent.append((copy, None))
        else:
            pl.when(when)(copy.start)
            sent.append((copy, when))
        return copy

    def send(ref, device, when=None):
        return post(ref, ref, device, when)

    loads[0].wait()
    loads[1].wait()
    own2r[...] = jnp.transpose(own2[...].astype(F32)).astype(BF16)
    mine = y * 2 + c
    spread = []
    for dy in (1, 3, 2, 0):
        for dc in range(2):
            first = pl.multiple_of(yo(dy) * 48, 16)
            if dy + dc == 0:
                keep = [
                    pltpu.make_async_copy(own1.at[pl.ds(first, 48)], parts1.at[mine], local_sem.at[11]),
                    pltpu.make_async_copy(own2r.at[pl.ds(first, 48)], parts2.at[mine], local_sem.at[12]),
                ]
                for copy in keep:
                    copy.start()
            else:
                to = dev(x, yo(dy), z, (c + dc) % 2)
                spread.append(post(own1.at[pl.ds(first, 48)], parts1.at[mine], to))
                spread.append(post(own2r.at[pl.ds(first, 48)], parts2.at[mine], to))

    loads[2].wait()
    halo = [
        post(rows.at[pl.ds(EDGE, EDGE)], rows.at[pl.ds(EDGE + ROWS, EDGE)], prev_dev),
        post(rows.at[pl.ds(ROWS, EDGE)], rows.at[pl.ds(0, EDGE)], next_dev),
    ]

    for copy in keep:
        copy.wait()
    for copy in spread:
        copy.wait_recv()
    full1 = jnp.concatenate([parts1[i].astype(F32) for i in range(8)], axis=1).astype(BF16)
    full2 = jnp.concatenate([parts2[i].astype(F32) for i in range(8)], axis=1).astype(BF16)
    for third in range(3):
        for p in range(2):
            j = 128 * (3 * p + third)
            weights[third, p, x, z, y] = full1[:, j : j + 128]
        weights[third, 2, x, z, y] = full2[:, 128 * third : 128 * third + 128]

    first_c = send(weights.at[2, :, x, z, y], x_dev)
    far_c = send(weights.at[2, :, x, z, y], dev(xo(2), y, z, c), c == 0)
    near = [
        send(weights.at[third, :, x, z, y], dev(x, y, zo(s * k), c))
        for k in (1, 2, 3)
        for third in (0, 1)
    ]
    far = send(weights.at[c, :, x, z, y], dev(x, y, zo(4), c))

    loads[3].wait()
    loads[4].wait()

    gain_row = jnp.concatenate([gain_v[i : i + 1, :] for i in range(12)], axis=1)
    bias_row = jnp.concatenate([bias_v[i : i + 1, :] for i in range(12)], axis=1)

    def norm(r0, n):
        v = rows[pl.ds(r0, n), :].astype(F32)
        mean = jnp.sum(v, axis=1, keepdims=True) * (1.0 / D)
        v = v - mean
        var = jnp.sum(v * v, axis=1, keepdims=True) * (1.0 / D)
        normed[pl.ds(r0, n), :] = (
            v * lax.rsqrt(var + EPSILON) * gain_row + bias_row
        ).astype(BF16)

    @pl.loop(0, 8)
    def _(i):
        norm(pl.multiple_of(EDGE + i * 32, 16), 32)

    first_c.wait_recv()
    mirrors_c = [send(weights.at[2, :, xo(-s), z, y], sibling)]
    pl.when(c == 0)(far_c.wait_recv)
    mirror_far_c = send(weights.at[2, :, xo(2), z, y], sibling, c == 0)
    mirrors = [[], []]
    for i, k in enumerate((1, 2, 3)):
        for third in (0, 1):
            near[2 * i + third].wait_recv()
            mirrors[third].append(send(weights.at[third, :, x, zo(-s * k), y], sibling))
    far.wait_recv()
    mirror_far = send(weights.at[c, :, x, zo(4), y], sibling)

    mirrors_c[0].wait_recv()
    pl.when(c == 1)(mirror_far_c.wait_recv)
    line_c = send(weights.at[2, :, :, z, y], y_dev)
    for third in (0, 1):
        for copy in mirrors[third]:
            copy.wait_recv()
    mirror_far.wait_recv()
    line_a = send(weights.at[0, :, x, :, y], y_dev)
    line_b = send(weights.at[1, :, x, :, y], x_dev)

    @pl.loop(8, 16)
    def _(i):
        norm(pl.multiple_of(EDGE + i * 32, 16), 32)

    hz = pl.ds(pl.multiple_of(4 * c, 4), 4)
    hx = pl.ds(pl.multiple_of(2 * c, 2), 2)
    line_c.wait_recv()
    line2_c = send(weights.at[2, :, hx, z, yo(-s)], y_dev)
    m_c1 = send(weights.at[2, :, :, z, yo(-s)], sibling)
    line_a.wait_recv()
    line2_a = send(weights.at[0, :, x, hz, yo(-s)], y_dev)
    m_a1 = send(weights.at[0, :, x, :, yo(-s)], sibling)
    line_b.wait_recv()
    line2_b = send(weights.at[1, :, xo(-s), hz, y], x_dev)
    m_b1 = send(weights.at[1, :, xo(-s), :, y], sibling)

    for copy in halo:
        copy.wait_recv()
    norm(0, EDGE)
    norm(EDGE + ROWS, EDGE)

    for load in loads[5:]:
        load.wait()
    base = (block * 4) % 8 + 8
    for i in range(6):
        q = base + i - 1
        there = block * 4 + i - 1
        row = seg_raw[pl.ds(q, 1), :].astype(F32)
        row = jnp.where(jnp.logical_or(there < 0, there >= 1024), -1.0, row)
        seg_col[pl.ds(128 * i, 128), :] = jnp.transpose(jnp.broadcast_to(row, (128, 128)))

    @pl.loop(0, 16)
    def _(i):
        r0 = pl.multiple_of(i * 32, 32)
        center = seg_col[pl.ds(r0 + 128, 32), :]
        low = jnp.zeros((32, 128), F32)
        high = jnp.zeros((32, 128), F32)
        for d in range(1, HALF + 1):
            low = low + jnp.where(seg_col[pl.ds(r0 + 128 - d, 32), :] == center, 1.0, 0.0)
            high = high + jnp.where(seg_col[pl.ds(r0 + 128 + d, 32), :] == center, 1.0, 0.0)
        before[pl.ds(r0, 32), :] = low
        after[pl.ds(r0, 32), :] = high

    line2_c.wait_recv()
    m_c2 = send(weights.at[2, :, hx, z, yo(-2 * s)], sibling)
    line2_a.wait_recv()
    m_a2 = send(weights.at[0, :, x, hz, yo(-2 * s)], sibling)
    line2_b.wait_recv()
    m_b2 = send(weights.at[1, :, xo(-2 * s), hz, y], sibling)

    order = (0, -1, 1, 2)

    def a_line(p, px, i):
        return weights.at[0, p, px, :, yo(s * order[i])]

    def a_half(p, px, i):
        return weights.at[0, p, px, hz, yo(s * order[i])]

    def b_line(p, py, i):
        return weights.at[1, p, xo(s * order[i]), :, py]

    def b_half(p, py, i):
        return weights.at[1, p, xo(s * order[i]), hz, py]

    def c_line(p, pz, i):
        return weights.at[2, p, :, pz, yo(s * order[i])]

    def c_half(p, pz, i):
        return weights.at[2, p, hx, pz, yo(s * order[i])]

    st = {}

    def own(p):
        st["a1", p], st["b1", p], st["c1", p] = [], [], []
        for i in range(4):
            if p == 0 and i == 2:
                m_a1.wait_recv()
                m_b1.wait_recv()
                m_c1.wait_recv()
            if p == 0 and i == 3:
                m_a2.wait_recv()
                m_b2.wait_recv()
                m_c2.wait_recv()
            st["c1", p].append(send(c_line(p, z, i), z_dev))
            st["a1", p].append(send(a_line(p, x, i), x_dev))
            st["b1", p].append(send(b_line(p, y, i), y_dev))

    def relay(p, i):
        if i == 0:
            st["a2", p], st["b2", p], st["c2", p] = [], [], []
        st["c1", p][i].wait_recv()
        st["c2", p].append(send(c_line(p, zo(-s), i), z_dev))
        st["a1", p][i].wait_recv()
        st["a2", p].append(send(a_half(p, xo(-s), i), x_dev))
        st["b1", p][i].wait_recv()
        st["b2", p].append(send(b_half(p, yo(-s), i), y_dev))
        if i == 3:
            st["ma1", p] = send(weights.at[0, p, xo(-s)], sibling)
            st["mb1", p] = send(weights.at[1, p, :, :, yo(-s)], sibling)
            st["mc1", p] = send(weights.at[2, p, :, zo(-s)], sibling)

    def c_step(p, k):
        nxt_k = []
        for i in range(4):
            st["c%d" % k, p][i].wait_recv()
            if k == 2:
                nxt_k.append(send(c_line(p, zo(-2 * s), i), z_dev))
            elif k == 3:
                nxt_k.append(send(c_half(p, zo(-3 * s), i), z_dev))
        st["c%d" % (k + 1), p] = nxt_k
        if k < 4:
            st["mc%d" % k, p] = send(weights.at[2, p, :, zo(-k * s)], sibling)
        else:
            st["mc%d" % k, p] = send(weights.at[2, p, hx, zo(4)], sibling)

    def ab_end(p):
        for i in range(4):
            st["a2", p][i].wait_recv()
        st["ma2", p] = send(weights.at[0, p, xo(2), hz], sibling)
        for i in range(4):
            st["b2", p][i].wait_recv()
        st["mb2", p] = send(weights.at[1, p, :, hz, yo(2)], sibling)

    def have_a(p):
        st["ma1", p].wait_recv()
        st["ma2", p].wait_recv()

    def have_b(p):
        st["mb1", p].wait_recv()
        st["mb2", p].wait_recv()

    def have_c(p):
        for k in range(1, 5):
            st["mc%d" % k, p].wait_recv()

    def expand(p, t):
        rhs = jnp.concatenate(
            [weights[t, p, g].reshape(D, 128) for g in (0, 1, 2, 3)], axis=1
        )
        both = jnp.dot(normed[...], rhs, preferred_element_type=F32)
        units = both[:, :256] * sigmoid(both[:, 256:])
        units = units.astype(BF16).astype(F32)
        gated[0] = units[:, :128]
        gated[1] = units[:, 128:]

    def conv(p, t, quarter):
        @pl.loop(4 * quarter, 4 * quarter + 4)
        def _(i):
            r0 = pl.multiple_of(i * 32, 32)
            low = before[pl.ds(r0, 32), :]
            high = after[pl.ds(r0, 32), :]
            sums = [None, None]
            for o in range(TAPS):
                d = o - HALF
                keep = low >= float(-d) if d < 0 else high >= float(d)
                for g in range(2):
                    ch = 768 * g + 128 * (3 * p + t)
                    v = gated[g, pl.ds(r0 + o + 1, 32), :]
                    if d != 0:
                        v = jnp.where(keep, v, 0.0)
                    v = v * taps_v[o : o + 1, ch : ch + 128]
                    sums[g] = v if sums[g] is None else sums[g] + v
            for g in range(2):
                l = 6 * g + 3 * p + t
                ch = 128 * l
                h = sums[g] * scale_v[l : l + 1, :] + shift_v[l : l + 1, :]
                active[pl.ds(r0, 32), ch : ch + 128] = (h * sigmoid(h)).astype(BF16)

    def unit(p, t, events):
        expand(p, t)
        if events:
            events.pop(0)()
        for quarter in range(4):
            conv(p, t, quarter)
            if events:
                events.pop(0)()

    own(0)
    for i in range(4):
        relay(0, i)
    own(1)
    c_step(0, 2)
    ab_end(0)
    have_a(0)
    E = functools.partial
    events = [E(c_step, 0, 3)] + [E(relay, 1, i) for i in range(4)] + [
        E(own, 2), E(c_step, 0, 4), E(c_step, 1, 2), E(ab_end, 1),
    ]
    unit(0, 0, events)
    have_b(0)
    unit(0, 1, events)
    for e in events:
        e()
    have_c(0)
    events = [E(relay, 2, i) for i in range(4)] + [
        E(c_step, 1, 3), E(c_step, 1, 4), E(c_step, 2, 2), E(ab_end, 2), E(c_step, 2, 3), E(c_step, 2, 4)
    ]
    unit(0, 2, events)
    have_a(1)
    unit(1, 0, events)
    have_b(1)
    for e in events:
        e()
    events = []
    unit(1, 1, events)
    have_c(1)
    unit(1, 2, events)
    have_a(2)
    have_b(2)
    have_c(2)
    stores = []
    for g in range(NX):
        rhs = jnp.concatenate([weights[t, 2, g].reshape(D, 128) for t in range(3)], axis=1)
        cols = pl.ds(384 * g, 384)
        product = jnp.dot(active[...], rhs, preferred_element_type=F32)
        result[:, cols] = (product + rows[pl.ds(EDGE, ROWS), cols].astype(F32)).astype(BF16)
        store = pltpu.make_async_copy(result.at[:, cols], out.at[:, cols], local_sem.at[13 + g])
        store.start()
        stores.append(store)
    for copy, when in sent:
        if when is None:
            copy.wait_send()
        else:
            pl.when(when)(copy.wait_send)
    for store in stores:
        store.wait()


def local(frames, segments, norm_gain, norm_bias, expand_weight, conv_kernel, batch_scale, batch_shift, project_weight):
    return pl.pallas_call(
        kernel,
        out_shape=jax.ShapeDtypeStruct((ROWS, D), BF16),
        in_specs=[pl.BlockSpec(memory_space=pltpu.HBM)] * 9,
        out_specs=pl.BlockSpec(memory_space=pltpu.HBM),
        scratch_shapes=[
            pltpu.VMEM((3, 3, NX, NZ, NY, 48, 128), BF16),
            pltpu.VMEM((ALL, D), BF16),
            pltpu.VMEM((ALL, D), BF16),
            pltpu.VMEM((ROWS, D), BF16),
            pltpu.VMEM((ROWS, D), BF16),
            pltpu.VMEM((2, ALL, 128), F32),
            pltpu.VMEM((24, 128), jnp.int32),
            pltpu.VMEM((768, 128), F32),
            pltpu.VMEM((ROWS, 128), F32),
            pltpu.VMEM((ROWS, 128), F32),
            pltpu.VMEM((192, 96), BF16),
            pltpu.VMEM((48, 192), BF16),
            pltpu.VMEM((192, 48), BF16),
            pltpu.VMEM((8, 48, 96), BF16),
            pltpu.VMEM((8, 48, 48), BF16),
            pltpu.VMEM((12, 128), F32),
            pltpu.VMEM((12, 128), F32),
            pltpu.VMEM((TAPS, D), F32),
            pltpu.VMEM((12, 128), F32),
            pltpu.VMEM((12, 128), F32),
            pltpu.SemaphoreType.DMA((20,)),
            pltpu.SemaphoreType.DMA((SEMS,)),
            pltpu.SemaphoreType.DMA((SEMS,)),
        ],
        compiler_params=pltpu.CompilerParams(
            collective_id=0, has_side_effects=True, vmem_limit_bytes=60 << 20
        ),
        name="conformer",
    )(
        frames,
        segments.reshape(1024, 128),
        norm_gain.reshape(12, 128),
        norm_bias.reshape(12, 128),
        expand_weight,
        conv_kernel,
        batch_scale.reshape(12, 128),
        batch_shift.reshape(12, 128),
        project_weight.T,
    )


def solution(mesh):
    in_specs = (
        P(("dp", "fsdp"), None),
        P(),
        P(),
        P(),
        P("fsdp", "dp"),
        P(),
        P(),
        P(),
        P("fsdp", "dp"),
    )
    out_specs = P(("dp", "fsdp"), None)
    return jax.shard_map(local, mesh=mesh, in_specs=in_specs, out_specs=out_specs, check_vma=False)
```

```python
import functools

import jax
import jax.numpy as jnp
from jax import lax
from jax.experimental import pallas as pl
from jax.experimental.pallas import tpu as pltpu
from jax.sharding import PartitionSpec as P

EPSILON = 1e-05
MESH = pl.DeviceIdType.MESH
F32 = jnp.float32
BF16 = jnp.bfloat16

NX, NY, NZ = 4, 4, 8
ROWS = 512
EDGE = 16
ALL = ROWS + 2 * EDGE
D = 1536
HALF = 15
TAPS = 31
SEMS = 256


def sigmoid(v):
    return 0.5 * jnp.tanh(0.5 * v) + 0.5


def kernel(
    frames, segs, gain, bias, w1, taps, scale, shift, w2, out,
    wide, late, rows, normed, active, result, gated, seg_raw, seg_col, before, after,
    own1, own2, own2r, parts1, parts2, gain_v, bias_v, taps_v, scale_v, shift_v,
    local_sem, send_sem, recv_sem,
):
    dp = lax.axis_index("dp")
    z = lax.axis_index("fsdp")
    x = dp // 8
    y = (dp // 2) % 4
    c = dp % 2
    s = 1 - 2 * c
    block = dp * 8 + z

    def dev(px, py, pz, pc):
        return (px * 8 + py * 2 + pc, pz)

    def xo(k):
        return (x + k + 2 * NX) % NX

    def yo(k):
        return (y + k + 2 * NY) % NY

    def zo(k):
        return (z + k + 2 * NZ) % NZ

    nxt = (block + 1) % 256
    prv = (block + 255) % 256
    next_dev = (nxt // 8, nxt % 8)
    prev_dev = (prv // 8, prv % 8)
    sibling = dev(x, y, z, 1 - c)
    x_dev = dev(xo(s), y, z, c)
    y_dev = dev(x, yo(s), z, c)
    z_dev = dev(x, y, zo(s), c)

    u = jnp.where(c == 0, x, y)
    v = jnp.where(c == 0, y, x)

    def m4(k):
        return (k + 8) % 4

    def uv_dev(pu, pv):
        return dev(jnp.where(c == 0, pu, pv), jnp.where(c == 0, pv, pu), z, c)

    tile0 = block // 2
    seg_tiles = [
        jnp.maximum(tile0 - 1, 0),
        tile0,
        jnp.minimum(tile0 + 1, 127),
    ]
    loads = [
        pltpu.make_async_copy(w1, own1, local_sem.at[0]),
        pltpu.make_async_copy(w2, own2, local_sem.at[1]),
        pltpu.make_async_copy(frames, rows.at[pl.ds(EDGE, ROWS)], local_sem.at[2]),
        pltpu.make_async_copy(gain, gain_v, local_sem.at[3]),
        pltpu.make_async_copy(bias, bias_v, local_sem.at[4]),
        pltpu.make_async_copy(taps, taps_v, local_sem.at[5]),
        pltpu.make_async_copy(scale, scale_v, local_sem.at[6]),
        pltpu.make_async_copy(shift, shift_v, local_sem.at[7]),
    ] + [
        pltpu.make_async_copy(
            segs.at[pl.ds(pl.multiple_of(t * 8, 8), 8)],
            seg_raw.at[pl.ds(8 * i, 8)],
            local_sem.at[8 + i],
        )
        for i, t in enumerate(seg_tiles)
    ]
    for load in loads:
        load.start()

    barrier = pltpu.get_barrier_semaphore()
    peers = [
        dev(x, yo(dy), z, (c + dc) % 2) for dy in range(NY) for dc in range(2) if dy + dc
    ]
    peers += [dev(x, y, zo(k), c) for k in range(1, NZ)]
    peers += [dev(xo(k), y, z, c) for k in range(1, NX)]
    peers += [next_dev, prev_dev]
    for peer in peers:
        pl.semaphore_signal(barrier, inc=1, device_id=peer, device_id_type=MESH)
    pl.semaphore_wait(barrier, len(peers))

    count = [0]
    sent = []

    def post(src, dst, device, when=None):
        i = count[0]
        count[0] += 1
        copy = pltpu.make_async_remote_copy(
            src_ref=src, dst_ref=dst, send_sem=send_sem.at[i], recv_sem=recv_sem.at[i],
            device_id=device, device_id_type=MESH,
        )
        if when is None:
            copy.start()
            sent.append((copy, None))
        else:
            pl.when(when)(copy.start)
            sent.append((copy, when))
        return copy

    def send(ref, device, when=None):
        return post(ref, ref, device, when)

    def mirror(ref, when=None):
        return send(ref, sibling, when)

    hz = [pl.ds(0, 4), pl.ds(4, 4)]
    hx = pl.ds(pl.multiple_of(2 * c, 2), 2)
    rest = pl.ds(1, 2)
    order = (0, -1, 1, 2)

    def wait(key):
        for copy in st[key]:
            copy.wait_recv()

    def line(p, pu, i, zz=slice(None)):
        return wide.at[c, p, pu, zz, m4(v + order[i])]

    def z_direct(p, key):
        st[key] = [
            send(wide.at[c, p, u, z, v], dev(x, y, zo(k), c)) for k in (4, 3, -3, 2, -2, 1, -1)
        ]

    def u_line(p, i):
        st.setdefault(("um", p), []).append(send(line(p, u, i), uv_dev(m4(u + 1), v)))
        st.setdefault(("up", p), []).append(send(line(p, u, i), uv_dev(m4(u - 1), v)))

    def v_first():
        wait("z0")
        st["v0"] = [send(wide.at[c, 0, u, :, v], uv_dev(u, m4(v + k))) for k in (1, -1, 2)]
        u_line(0, 0)
        z_direct(rest, "zr")

    def v_rest():
        wait("zr")
        st["vr"] = [send(wide.at[c, rest, u, :, v], uv_dev(u, m4(v + k))) for k in (1, -1)]

    def u_first(i):
        st["v0"][i - 1].wait_recv()
        u_line(0, i)
        if i == 3:
            st["m", 0] = [mirror(wide.at[c, 0, u])]

    def v_relay():
        st["vr"][0].wait_recv()
        a = send(wide.at[c, rest, u, hz[0], m4(v - 1)], uv_dev(u, m4(v + 1)))
        st["vr"][1].wait_recv()
        b = send(wide.at[c, rest, u, hz[1], m4(v + 1)], uv_dev(u, m4(v - 1)))
        st["vr2"] = [a, b]

    def u_lines(p):
        for i in range(3):
            u_line(p, i)
        if p == 1:
            wait("vr2")
        u_line(p, 3)
        st["m", p] = [mirror(wide.at[c, p, u])]

    def relay(p, i):
        halves = st.setdefault(("h", p), [])
        st["um", p][i].wait_recv()
        halves.append(send(line(p, m4(u - 1), i, hz[0]), uv_dev(m4(u + 1), v)))
        st["up", p][i].wait_recv()
        halves.append(send(line(p, m4(u + 1), i, hz[1]), uv_dev(m4(u - 1), v)))
        if i == 3:
            st["m", p].append(mirror(wide.at[c, p, m4(u - 1)]))
            st["m", p].append(mirror(wide.at[c, p, m4(u + 1)]))

    def u_end(p):
        wait(("h", p))
        st["m", p].append(mirror(wide.at[c, p, m4(u + 2)]))

    def c_first():
        st["cx"] = send(late.at[:, x, z, y], x_dev)
        st["cx2"] = send(late.at[:, x, z, y], dev(xo(2), y, z, c), c == 0)

    def c_x():
        st["cx"].wait_recv()
        st["cmx"] = mirror(late.at[:, xo(-s), z, y])
        pl.when(c == 0)(st["cx2"].wait_recv)
        st["cmx2"] = mirror(late.at[:, xo(2), z, y], c == 0)

    def c_line(pz, i, xx=slice(None)):
        return late.at[:, xx, pz, yo(s * order[i])]

    def c_y():
        st["cmx"].wait_recv()
        pl.when(c == 1)(st["cmx2"].wait_recv)
        st["cy"] = send(late.at[:, :, z, y], y_dev)
        st["cz", 1] = [send(c_line(z, 0), z_dev)]

    def c_y1():
        st["cy"].wait_recv()
        st["cy2"] = send(late.at[:, hx, z, yo(-s)], y_dev)
        st["cmy"] = mirror(late.at[:, :, z, yo(-s)])
        st["cz", 1].append(send(c_line(z, 1), z_dev))

    def c_y2():
        st["cmy"].wait_recv()
        st["cz", 1].append(send(c_line(z, 2), z_dev))
        st["cy2"].wait_recv()
        st["cmy2"] = mirror(late.at[:, hx, z, yo(2)])

    def c_y3():
        st["cmy2"].wait_recv()
        st["cz", 1].append(send(c_line(z, 3), z_dev))

    def c_z(k, i):
        st["cz", k][i].wait_recv()
        if k < 4:
            part = hx if k == 3 else slice(None)
            st.setdefault(("cz", k + 1), []).append(send(c_line(zo(-s * k), i, part), z_dev))
        if i == 3:
            if k < 4:
                st.setdefault("mc", []).append(mirror(late.at[:, :, zo(-s * k)]))
            else:
                st["mc"].append(mirror(late.at[:, hx, zo(4)]))

    loads[0].wait()
    loads[1].wait()
    own2r[...] = jnp.transpose(own2[...].astype(F32)).astype(BF16)
    mine = y * 2 + c
    spread = []
    for dy in (1, 3, 2, 0):
        for dc in range(2):
            first = pl.multiple_of(yo(dy) * 48, 16)
            if dy + dc == 0:
                keep = [
                    pltpu.make_async_copy(own1.at[pl.ds(first, 48)], parts1.at[mine], local_sem.at[11]),
                    pltpu.make_async_copy(own2r.at[pl.ds(first, 48)], parts2.at[mine], local_sem.at[12]),
                ]
                for copy in keep:
                    copy.start()
            else:
                to = dev(x, yo(dy), z, (c + dc) % 2)
                spread.append(post(own1.at[pl.ds(first, 48)], parts1.at[mine], to))
                spread.append(post(own2r.at[pl.ds(first, 48)], parts2.at[mine], to))

    loads[2].wait()
    halo = [
        post(rows.at[pl.ds(EDGE, EDGE)], rows.at[pl.ds(EDGE + ROWS, EDGE)], prev_dev),
        post(rows.at[pl.ds(ROWS, EDGE)], rows.at[pl.ds(0, EDGE)], next_dev),
    ]

    for copy in keep:
        copy.wait()
    for copy in spread:
        copy.wait_recv()
    full1 = jnp.concatenate([parts1[i].astype(F32) for i in range(8)], axis=1).astype(BF16)
    full2 = jnp.concatenate([parts2[i].astype(F32) for i in range(8)], axis=1).astype(BF16)
    for p in range(3):
        a = full1[:, 256 * p : 256 * p + 128]
        b = full1[:, 256 * p + 128 : 256 * p + 256]
        wide[c, p, u, z, v] = jnp.where(c == 0, a, b)
        late[p, x, z, y] = full2[:, 128 * p : 128 * p + 128]

    st = {}
    z_direct(0, "z0")
    c_first()

    loads[3].wait()
    loads[4].wait()

    gain_row = jnp.concatenate([gain_v[i : i + 1, :] for i in range(12)], axis=1)
    bias_row = jnp.concatenate([bias_v[i : i + 1, :] for i in range(12)], axis=1)

    def norm(r0, n):
        v = rows[pl.ds(r0, n), :].astype(F32)
        mean = jnp.sum(v, axis=1, keepdims=True) * (1.0 / D)
        v = v - mean
        var = jnp.sum(v * v, axis=1, keepdims=True) * (1.0 / D)
        normed[pl.ds(r0, n), :] = (
            v * lax.rsqrt(var + EPSILON) * gain_row + bias_row
        ).astype(BF16)

    @pl.loop(0, 8)
    def _(i):
        norm(pl.multiple_of(EDGE + i * 32, 16), 32)

    v_first()
    c_x()
    c_y()

    @pl.loop(8, 16)
    def _(i):
        norm(pl.multiple_of(EDGE + i * 32, 16), 32)

    u_first(1)
    u_first(2)
    u_first(3)
    v_rest()
    c_y1()

    for copy in halo:
        copy.wait_recv()
    norm(0, EDGE)
    norm(EDGE + ROWS, EDGE)

    for load in loads[5:]:
        load.wait()
    base = (block * 4) % 8 + 8
    for i in range(6):
        q = base + i - 1
        there = block * 4 + i - 1
        row = seg_raw[pl.ds(q, 1), :].astype(F32)
        row = jnp.where(jnp.logical_or(there < 0, there >= 1024), -1.0, row)
        seg_col[pl.ds(128 * i, 128), :] = jnp.transpose(jnp.broadcast_to(row, (128, 128)))

    @pl.loop(0, 16)
    def _(i):
        r0 = pl.multiple_of(i * 32, 32)
        center = seg_col[pl.ds(r0 + 128, 32), :]
        low = jnp.zeros((32, 128), F32)
        high = jnp.zeros((32, 128), F32)
        for d in range(1, HALF + 1):
            low = low + jnp.where(seg_col[pl.ds(r0 + 128 - d, 32), :] == center, 1.0, 0.0)
            high = high + jnp.where(seg_col[pl.ds(r0 + 128 + d, 32), :] == center, 1.0, 0.0)
        before[pl.ds(r0, 32), :] = low
        after[pl.ds(r0, 32), :] = high

    v_relay()
    c_y2()
    relay(0, 0)
    relay(0, 1)
    c_y3()
    relay(0, 2)
    relay(0, 3)
    u_lines(1)
    c_z(1, 0)
    c_z(1, 1)
    u_end(0)
    relay(1, 0)
    c_z(1, 2)

    def operand(m, p, g):
        if m == 0:
            return wide[0, p, g].reshape(D, 128)
        return jnp.concatenate([wide[1, p, k % 4, k // 4, g] for k in range(32)], axis=0)

    def expand(p, g):
        rhs = jnp.concatenate([operand(m, p, g + h) for h in (0, 2) for m in (0, 1)], axis=1)
        both = jnp.dot(normed[...], rhs, preferred_element_type=F32)
        units = both[:, :256] * sigmoid(both[:, 256:])
        units = units.astype(BF16).astype(F32)
        gated[2 * g] = units[:, :128]
        gated[2 * g + 1] = units[:, 128:]

    def conv(p, eighth):
        tiles = [6 * g + 2 * p + m for g in range(2) for m in range(2)]

        @pl.loop(2 * eighth, 2 * eighth + 2)
        def _(i):
            r0 = pl.multiple_of(i * 32, 32)
            low = before[pl.ds(r0, 32), :]
            high = after[pl.ds(r0, 32), :]
            sums = [None] * 4
            for o in range(TAPS):
                d = o - HALF
                keep = low >= float(-d) if d < 0 else high >= float(d)
                for i, l in enumerate(tiles):
                    t = gated[i, pl.ds(r0 + o + 1, 32), :]
                    if d != 0:
                        t = jnp.where(keep, t, 0.0)
                    t = t * taps_v[o : o + 1, 128 * l : 128 * l + 128]
                    sums[i] = t if sums[i] is None else sums[i] + t
            for i, l in enumerate(tiles):
                h = sums[i] * scale_v[l : l + 1, :] + shift_v[l : l + 1, :]
                active[pl.ds(r0, 32), 128 * l : 128 * l + 128] = (h * sigmoid(h)).astype(BF16)

    def serve(events):
        if events:
            events.pop(0)()

    def columns(p, events):
        for copy in st["m", p]:
            copy.wait_recv()
        for g in range(2):
            expand(p, g)
            serve(events)
        for eighth in range(8):
            conv(p, eighth)
            serve(events)

    E = functools.partial
    events = [
        E(relay, 1, 1), E(c_z, 1, 3), E(relay, 1, 2), E(relay, 1, 3), E(u_lines, 2), E(c_z, 2, 0),
        E(c_z, 2, 1), E(u_end, 1), E(relay, 2, 0), E(c_z, 2, 2),
    ]
    columns(0, events)
    events = [
        E(relay, 2, 1), E(c_z, 2, 3), E(relay, 2, 2), E(c_z, 3, 0), E(relay, 2, 3), E(c_z, 3, 1),
        E(u_end, 2), E(c_z, 3, 2), E(c_z, 3, 3),
    ]
    columns(1, events)
    events = [E(c_z, 4, i) for i in range(4)]
    columns(2, events)
    for copy in st["mc"]:
        copy.wait_recv()
    stores = []
    for g in range(NX):
        rhs = jnp.concatenate([late[t, g].reshape(D, 128) for t in range(3)], axis=1)
        cols = pl.ds(384 * g, 384)
        product = jnp.dot(active[...], rhs, preferred_element_type=F32)
        result[:, cols] = (product + rows[pl.ds(EDGE, ROWS), cols].astype(F32)).astype(BF16)
        store = pltpu.make_async_copy(result.at[:, cols], out.at[:, cols], local_sem.at[13 + g])
        store.start()
        stores.append(store)
    for copy, when in sent:
        if when is None:
            copy.wait_send()
        else:
            pl.when(when)(copy.wait_send)
    for store in stores:
        store.wait()


def local(frames, segments, norm_gain, norm_bias, expand_weight, conv_kernel, batch_scale, batch_shift, project_weight):
    return pl.pallas_call(
        kernel,
        out_shape=jax.ShapeDtypeStruct((ROWS, D), BF16),
        in_specs=[pl.BlockSpec(memory_space=pltpu.HBM)] * 9,
        out_specs=pl.BlockSpec(memory_space=pltpu.HBM),
        scratch_shapes=[
            pltpu.VMEM((2, 3, 4, NZ, 4, 48, 128), BF16),
            pltpu.VMEM((3, NX, NZ, NY, 48, 128), BF16),
            pltpu.VMEM((ALL, D), BF16),
            pltpu.VMEM((ALL, D), BF16),
            pltpu.VMEM((ROWS, D), BF16),
            pltpu.VMEM((ROWS, D), BF16),
            pltpu.VMEM((4, ALL, 128), F32),
            pltpu.VMEM((24, 128), jnp.int32),
            pltpu.VMEM((768, 128), F32),
            pltpu.VMEM((ROWS, 128), F32),
            pltpu.VMEM((ROWS, 128), F32),
            pltpu.VMEM((192, 96), BF16),
            pltpu.VMEM((48, 192), BF16),
            pltpu.VMEM((192, 48), BF16),
            pltpu.VMEM((8, 48, 96), BF16),
            pltpu.VMEM((8, 48, 48), BF16),
            pltpu.VMEM((12, 128), F32),
            pltpu.VMEM((12, 128), F32),
            pltpu.VMEM((TAPS, D), F32),
            pltpu.VMEM((12, 128), F32),
            pltpu.VMEM((12, 128), F32),
            pltpu.SemaphoreType.DMA((20,)),
            pltpu.SemaphoreType.DMA((SEMS,)),
            pltpu.SemaphoreType.DMA((SEMS,)),
        ],
        compiler_params=pltpu.CompilerParams(
            collective_id=0, has_side_effects=True, vmem_limit_bytes=60 << 20
        ),
        name="conformer",
    )(
        frames,
        segments.reshape(1024, 128),
        norm_gain.reshape(12, 128),
        norm_bias.reshape(12, 128),
        expand_weight,
        conv_kernel,
        batch_scale.reshape(12, 128),
        batch_shift.reshape(12, 128),
        project_weight.T,
    )


def solution(mesh):
    in_specs = (
        P(("dp", "fsdp"), None),
        P(),
        P(),
        P(),
        P("fsdp", "dp"),
        P(),
        P(),
        P(),
        P("fsdp", "dp"),
    )
    out_specs = P(("dp", "fsdp"), None)
    return jax.shard_map(local, mesh=mesh, in_specs=in_specs, out_specs=out_specs, check_vma=False)
```

```python
import functools

import jax
import jax.numpy as jnp
from jax import lax
from jax.experimental import pallas as pl
from jax.experimental.pallas import tpu as pltpu
from jax.sharding import PartitionSpec as P

EPSILON = 1e-05
MESH = pl.DeviceIdType.MESH
F32 = jnp.float32
BF16 = jnp.bfloat16

NX, NY, NZ = 4, 4, 8
ROWS = 512
EDGE = 16
ALL = ROWS + 2 * EDGE
D = 1536
HALF = 15
TAPS = 31
SEMS = 256


def sigmoid(v):
    return 0.5 * jnp.tanh(0.5 * v) + 0.5


def kernel(
    frames, segs, gain, bias, w1, taps, scale, shift, w2, out,
    wide, late, rows, normed, active, result, wider, gated, seg_raw, seg_col, before, after,
    own1, own2, pack1, pack2, parts1, parts2, gain_v, bias_v, taps_v, scale_v, shift_v,
    local_sem, part_send, part_recv, send_sem, recv_sem,
):
    dp = lax.axis_index("dp")
    z = lax.axis_index("fsdp")
    x = dp // 8
    y = (dp // 2) % 4
    c = dp % 2
    s = 1 - 2 * c
    block = dp * 8 + z

    def dev(px, py, pz, pc):
        return (px * 8 + py * 2 + pc, pz)

    def xo(k):
        return (x + k + 2 * NX) % NX

    def yo(k):
        return (y + k + 2 * NY) % NY

    def zo(k):
        return (z + k + 2 * NZ) % NZ

    nxt = (block + 1) % 256
    prv = (block + 255) % 256
    next_dev = (nxt // 8, nxt % 8)
    prev_dev = (prv // 8, prv % 8)

    u = jnp.where(c == 0, x, y)
    v = jnp.where(c == 0, y, x)

    def m4(k):
        return (k + 8) % 4

    def uv_dev(pu, pv):
        return dev(jnp.where(c == 0, pu, pv), jnp.where(c == 0, pv, pu), z, c)

    tile0 = block // 2
    seg_tiles = [
        jnp.maximum(tile0 - 1, 0),
        tile0,
        jnp.minimum(tile0 + 1, 127),
    ]
    loads = [
        pltpu.make_async_copy(w1, own1, local_sem.at[0]),
        pltpu.make_async_copy(w2, own2, local_sem.at[1]),
        pltpu.make_async_copy(frames, rows.at[pl.ds(EDGE, ROWS)], local_sem.at[2]),
        pltpu.make_async_copy(gain, gain_v, local_sem.at[3]),
        pltpu.make_async_copy(bias, bias_v, local_sem.at[4]),
        pltpu.make_async_copy(taps, taps_v, local_sem.at[5]),
        pltpu.make_async_copy(scale, scale_v, local_sem.at[6]),
        pltpu.make_async_copy(shift, shift_v, local_sem.at[7]),
    ] + [
        pltpu.make_async_copy(
            segs.at[pl.ds(pl.multiple_of(t * 8, 8), 8)],
            seg_raw.at[pl.ds(8 * i, 8)],
            local_sem.at[8 + i],
        )
        for i, t in enumerate(seg_tiles)
    ]
    for load in loads:
        load.start()

    barrier = pltpu.get_barrier_semaphore()
    peers = [
        dev(x, yo(dy), z, (c + dc) % 2) for dy in range(NY) for dc in range(2) if dy + dc
    ]
    peers += [dev(x, y, zo(k), c) for k in range(1, NZ)]
    peers += [dev(xo(k), y, z, c) for k in range(1, NX)]
    peers += [next_dev, prev_dev]
    for peer in peers:
        pl.semaphore_signal(barrier, inc=1, device_id=peer, device_id_type=MESH)
    pl.semaphore_wait(barrier, len(peers))

    count = [0]
    sent = []

    class Copy:
        def __init__(self, src, dst, device, when=None, heard=None):
            self.src, self.dst, self.device, self.when, self.heard = src, dst, device, when, heard
            self.i = count[0]
            count[0] += 1
            sent.append(self)
            self._on(when, "start")

        def _on(self, when, method):
            def act():
                copy = pltpu.make_async_remote_copy(
                    src_ref=self.src(), dst_ref=self.dst(), send_sem=send_sem.at[self.i],
                    recv_sem=recv_sem.at[self.i], device_id=self.device(), device_id_type=MESH,
                )
                getattr(copy, method)()

            if when is None:
                act()
            else:
                pl.when(c == when)(act)

        def wait_recv(self):
            self._on(self.heard, "wait_recv")

        def wait_send(self):
            self._on(self.when, "wait_send")

    def drain():
        while sent:
            sent.pop(0).wait_send()

    def send(ref, device, when=None, heard=None):
        return Copy(ref, ref, device, when, heard)

    def to_sibling():
        return dev(x, y, z, 1 - c)

    def mirror(ref, when=None, heard=None):
        return send(ref, to_sibling, when, heard)

    hz = (pl.ds(0, 4), pl.ds(4, 4))
    whole = slice(None)
    rest = pl.ds(1, 2)
    order = (0, -1, 1, 2)
    st = {}

    def hx():
        return pl.ds(pl.multiple_of(2 * c, 2), 2)

    def wait(key):
        for copy in st[key]:
            copy.wait_recv()

    def line(p, du, i, zz=whole):
        return lambda: wide.at[c, p, m4(u + du), zz, m4(v + order[i])]

    def u_to(k):
        return lambda: uv_dev(m4(u + k), v)

    def v_to(k):
        return lambda: uv_dev(u, m4(v + k))

    def plane(p, du):
        return lambda: wide.at[c, p, m4(u + du)]

    def z_direct(p, key):
        st[key] = [
            send(lambda: wide.at[c, p, u, z, v], lambda k=k: dev(x, y, zo(k), c))
            for k in (4, 3, -3, 2, -2, 1, -1)
        ]

    def u_line(p, i):
        st.setdefault(("um", p), []).append(send(line(p, 0, i), u_to(1)))
        st.setdefault(("up", p), []).append(send(line(p, 0, i), u_to(-1)))

    def v_first():
        wait("z0")
        st["v0"] = [send(line(0, 0, 0), v_to(k)) for k in (1, -1, 2)]
        u_line(0, 0)
        z_direct(rest, "zr")

    def v_rest():
        wait("zr")
        st["vr"] = [send(line(rest, 0, 0), v_to(k)) for k in (1, -1)]

    def u_first(i):
        st["v0"][i - 1].wait_recv()
        u_line(0, i)
        if i == 3:
            st["m", 0] = [mirror(plane(0, 0))]

    def v_relay():
        st["vr"][0].wait_recv()
        a = send(line(rest, 0, 1, hz[0]), v_to(1))
        st["vr"][1].wait_recv()
        b = send(line(rest, 0, 2, hz[1]), v_to(-1))
        st["vr2"] = [a, b]

    def u_lines(p):
        for i in range(3):
            u_line(p, i)
        if p == 1:
            wait("vr2")
        u_line(p, 3)
        st["m", p] = [mirror(plane(p, 0))]

    def relay(p, i):
        halves = st.setdefault(("h", p), [])
        st["um", p][i].wait_recv()
        halves.append(send(line(p, -1, i, hz[0]), u_to(1)))
        st["up", p][i].wait_recv()
        halves.append(send(line(p, 1, i, hz[1]), u_to(-1)))
        if i == 3:
            st["m", p].append(mirror(plane(p, -1)))
            st["m", p].append(mirror(plane(p, 1)))

    def u_end(p):
        wait(("h", p))
        st["m", p].append(mirror(plane(p, 2)))

    def x_to():
        return dev(xo(s), y, z, c)

    def y_to():
        return dev(x, yo(s), z, c)

    def z_to():
        return dev(x, y, zo(s), c)

    def c_first():
        st["cx"] = send(lambda: late.at[:, x, z, y], x_to)
        st["cx2"] = send(lambda: late.at[:, x, z, y], lambda: dev(xo(2), y, z, c), 0, 0)

    def c_x():
        st["cx"].wait_recv()
        st["cmx"] = mirror(lambda: late.at[:, xo(-s), z, y])
        st["cx2"].wait_recv()
        st["cmx2"] = mirror(lambda: late.at[:, xo(2), z, y], 0, 1)

    def c_line(k, i, xx=None):
        return lambda: late.at[:, whole if xx is None else xx(), zo(-s * k), yo(s * order[i])]

    def c_y():
        st["cmx"].wait_recv()
        st["cmx2"].wait_recv()
        st["cy"] = send(c_line(0, 0), y_to)
        st["cz", 1] = [send(c_line(0, 0), z_to)]

    def c_y1():
        st["cy"].wait_recv()
        st["cy2"] = send(c_line(0, 1, hx), y_to)
        st["cmy"] = mirror(c_line(0, 1))
        st["cz", 1].append(send(c_line(0, 1), z_to))

    def c_y2():
        st["cmy"].wait_recv()
        st["cz", 1].append(send(c_line(0, 2), z_to))
        st["cy2"].wait_recv()
        st["cmy2"] = mirror(c_line(0, 3, hx))

    def c_y3():
        st["cmy2"].wait_recv()
        st["cz", 1].append(send(c_line(0, 3), z_to))

    def c_z(k, i):
        st["cz", k][i].wait_recv()
        if k < 4:
            part = hx if k == 3 else None
            st.setdefault(("cz", k + 1), []).append(send(c_line(k, i, part), z_to))
        if i == 3:
            if k < 4:
                st.setdefault("mc", []).append(mirror(lambda: late.at[:, :, zo(-s * k)]))
            else:
                st["mc"].append(mirror(lambda: late.at[:, hx(), zo(4)]))

    loads[0].wait()
    for k in range(4):
        pack1[k] = jnp.concatenate(
            [own1[48 * k : 48 * k + 48, :].astype(F32), jnp.zeros((48, 32), F32)], axis=1
        ).astype(BF16)
    home = y // 2
    slot = (y % 2) * 2 + c

    def part_copy(dy, core):
        return pltpu.make_async_remote_copy(
            src_ref=pack1.at[yo(dy)], dst_ref=parts1.at[slot], send_sem=part_send.at[dy],
            recv_sem=part_recv.at[2 * dy + core], device_id=dev(x, yo(dy), z, home), device_id_type=MESH,
        )

    for dy in (2, 1, 3):
        part_copy(dy, c).start()

    @pl.when(c == home)
    def _():
        parts1[slot] = pack1[y]

    @pl.when(c != home)
    def _():
        part_copy(0, c).start()

    loads[1].wait()
    own2r = jnp.transpose(own2[...].astype(F32))
    for k in range(4):
        pack2[k] = jnp.concatenate(
            [own2r[48 * k : 48 * k + 48, :], jnp.zeros((48, 80), F32)], axis=1
        ).astype(BF16)
    mine = y * 2 + c
    spread = []
    for dy, dc in ((2, 0), (2, 1), (1, 0), (3, 0), (1, 1), (3, 1), (0, 1)):
        spread.append(
            Copy(
                lambda dy=dy: pack2.at[yo(dy)],
                lambda: parts2.at[mine],
                lambda dy=dy, dc=dc: dev(x, yo(dy), z, (c + dc) % 2),
            )
        )
    parts2[mine] = pack2[y]

    for dy in range(4):
        for core in range(2):
            due = yo(-dy) // 2 == c
            if dy == 0:
                due = jnp.logical_and(due, c != core)

            @pl.when(due)
            def _(dy=dy, core=core):
                part_copy(dy, core).wait_recv()

    full1 = jnp.concatenate([parts1[i, :, :96].astype(F32) for i in range(4)], axis=1).astype(BF16)
    for p in range(3):
        wide[c, p, u, z, v] = full1[:, 128 * p : 128 * p + 128]
    z_direct(0, "z0")

    loads[2].wait()
    halo = [
        Copy(
            lambda: rows.at[pl.ds(EDGE, EDGE)], lambda: rows.at[pl.ds(EDGE + ROWS, EDGE)], lambda: prev_dev
        ),
        Copy(lambda: rows.at[pl.ds(ROWS, EDGE)], lambda: rows.at[pl.ds(0, EDGE)], lambda: next_dev),
    ]

    for copy in spread:
        copy.wait_recv()
    full2 = jnp.concatenate([parts2[i, :, :48].astype(F32) for i in range(8)], axis=1).astype(BF16)
    for p in range(3):
        late[p, x, z, y] = full2[:, 128 * p : 128 * p + 128]
    c_first()

    loads[3].wait()
    loads[4].wait()

    gain_row = jnp.concatenate([gain_v[i : i + 1, :] for i in range(12)], axis=1)
    bias_row = jnp.concatenate([bias_v[i : i + 1, :] for i in range(12)], axis=1)

    def norm(r0, n):
        v = rows[pl.ds(r0, n), :].astype(F32)
        mean = jnp.sum(v, axis=1, keepdims=True) * (1.0 / D)
        v = v - mean
        var = jnp.sum(v * v, axis=1, keepdims=True) * (1.0 / D)
        normed[pl.ds(r0, n), :] = (
            v * lax.rsqrt(var + EPSILON) * gain_row + bias_row
        ).astype(BF16)

    @pl.loop(0, 8)
    def _(i):
        norm(pl.multiple_of(EDGE + i * 32, 16), 32)

    v_first()
    c_x()
    c_y()

    @pl.loop(8, 16)
    def _(i):
        norm(pl.multiple_of(EDGE + i * 32, 16), 32)

    u_first(1)
    u_first(2)
    u_first(3)
    v_rest()
    c_y1()

    for copy in halo:
        copy.wait_recv()
    norm(0, EDGE)
    norm(EDGE + ROWS, EDGE)

    for load in loads[5:]:
        load.wait()
    base = (block * 4) % 8 + 8
    for i in range(6):
        q = base + i - 1
        there = block * 4 + i - 1
        row = seg_raw[pl.ds(q, 1), :].astype(F32)
        row = jnp.where(jnp.logical_or(there < 0, there >= 1024), -1.0, row)
        seg_col[pl.ds(128 * i, 128), :] = jnp.transpose(jnp.broadcast_to(row, (128, 128)))

    @pl.loop(0, 16)
    def _(i):
        r0 = pl.multiple_of(i * 32, 32)
        center = seg_col[pl.ds(r0 + 128, 32), :]
        low = jnp.zeros((32, 128), F32)
        high = jnp.zeros((32, 128), F32)
        for d in range(1, HALF + 1):
            low = low + jnp.where(seg_col[pl.ds(r0 + 128 - d, 32), :] == center, 1.0, 0.0)
            high = high + jnp.where(seg_col[pl.ds(r0 + 128 + d, 32), :] == center, 1.0, 0.0)
        before[pl.ds(r0, 32), :] = low
        after[pl.ds(r0, 32), :] = high

    v_relay()
    c_y2()
    relay(0, 0)
    relay(0, 1)
    c_y3()
    relay(0, 2)
    relay(0, 3)
    u_lines(1)
    c_z(1, 0)
    c_z(1, 1)
    u_end(0)
    relay(1, 0)
    c_z(1, 2)

    def operand(m, p, g):
        if m == 0:
            return wide[0, p, g].reshape(D, 128)
        return jnp.concatenate([wide[1, p, k % 4, k // 4, g] for k in range(32)], axis=0)

    def expand(p, g):
        rhs = jnp.concatenate([operand(m, p, g) for m in (0, 1)], axis=1)
        both = jnp.dot(normed[...], rhs, preferred_element_type=F32)
        for m in (0, 1):
            wider[g, m] = both[:, 128 * m : 128 * m + 128]

    def gate():
        @pl.loop(0, ALL // 32)
        def _(i):
            r = pl.ds(pl.multiple_of(i * 32, 32), 32)
            for g in (0, 1):
                for m in (0, 1):
                    t = wider[g, m, r, :] * sigmoid(wider[g + 2, m, r, :])
                    gated[2 * g + m, r, :] = t.astype(BF16).astype(F32)

    def conv(p, i):
        tiles = [6 * g + 3 * m + p for g in range(2) for m in range(2)]
        r0 = pl.multiple_of(i * 32, 32)
        low = before[pl.ds(r0, 32), :]
        high = after[pl.ds(r0, 32), :]
        sums = [None] * 4
        for o in range(TAPS):
            d = o - HALF
            keep = low >= float(-d) if d < 0 else high >= float(d)
            for k, l in enumerate(tiles):
                t = gated[k, pl.ds(r0 + o + 1, 32), :]
                if d != 0:
                    t = jnp.where(keep, t, 0.0)
                t = t * taps_v[o : o + 1, 128 * l : 128 * l + 128]
                sums[k] = t if sums[k] is None else sums[k] + t
        for k, l in enumerate(tiles):
            h = sums[k] * scale_v[l : l + 1, :] + shift_v[l : l + 1, :]
            h = (h * sigmoid(h)).astype(BF16)
            active[pl.ds(r0, 32), 512 * p + 128 * k : 512 * p + 128 * k + 128] = h

    def project(passes, source, g):
        tiles = [late[t, g].reshape(D, 128) for t in range(3)]
        starts = [128 * (6 * h + 3 * m + p) for p in passes for h in (0, 1) for m in (0, 1)]
        rhs = jnp.concatenate(
            [jnp.concatenate([t[a : a + 128] for a in starts], axis=0) for t in tiles], axis=1
        )
        return jnp.dot(source[...], rhs, preferred_element_type=F32)

    def quarters(body, slots):
        @pl.loop(0, 4)
        def _(j):
            body(j)
            for k, events in enumerate(slots):
                if events:

                    @pl.when(j == k)
                    def _(events=events):
                        for event in events:
                            event()

    E = functools.partial

    def conv_alone(p):
        def body(j):
            for q in range(4):
                conv(p, 4 * j + q)

        return body

    def expand_alone(p):
        return lambda j: expand(p, j)

    for dy in (1, 2, 3):
        part_copy(dy, c).wait_send()

    @pl.when(c != home)
    def _():
        part_copy(0, c).wait_send()

    wait(("m", 0))
    quarters(
        expand_alone(0), [[E(relay, 1, 1)], [E(c_z, 1, 3)], [E(relay, 1, 2)], [E(relay, 1, 3), E(u_lines, 2)]]
    )
    gate()
    quarters(
        conv_alone(0),
        [[E(c_z, 2, 0)], [E(c_z, 2, 1)], [E(u_end, 1), E(relay, 2, 0)], [E(c_z, 2, 2), E(relay, 2, 1)]],
    )
    wait(("m", 1))
    quarters(
        expand_alone(1), [[E(c_z, 2, 3)], [E(relay, 2, 2)], [E(c_z, 3, 0)], [E(relay, 2, 3), E(c_z, 3, 1)]]
    )
    gate()
    quarters(conv_alone(1), [[E(c_z, 3, 2)], [E(u_end, 2)], [E(c_z, 3, 3)], [E(c_z, 4, 0)]])
    wait(("m", 2))
    quarters(expand_alone(2), [[], [E(c_z, 4, 1)], [], [E(c_z, 4, 2)]])
    gate()
    quarters(conv_alone(2), [[E(c_z, 4, 3)], [], [], []])
    wait("mc")
    stores = []
    for g in range(NX):
        cols = pl.ds(384 * g, 384)
        product = project((0, 1, 2), active, g)
        result[:, cols] = (product + rows[pl.ds(EDGE, ROWS), cols].astype(F32)).astype(BF16)
        store = pltpu.make_async_copy(result.at[:, cols], out.at[:, cols], local_sem.at[13 + g])
        store.start()
        stores.append(store)
    drain()
    for store in stores:
        store.wait()


def local(frames, segments, norm_gain, norm_bias, expand_weight, conv_kernel, batch_scale, batch_shift, project_weight):
    return pl.pallas_call(
        kernel,
        out_shape=jax.ShapeDtypeStruct((ROWS, D), BF16),
        in_specs=[pl.BlockSpec(memory_space=pltpu.HBM)] * 9,
        out_specs=pl.BlockSpec(memory_space=pltpu.HBM),
        scratch_shapes=[
            pltpu.VMEM((2, 3, 4, NZ, 4, 48, 128), BF16),
            pltpu.VMEM((3, NX, NZ, NY, 48, 128), BF16),
            pltpu.VMEM((ALL, D), BF16),
            pltpu.VMEM((ALL, D), BF16),
            pltpu.VMEM((ROWS, D), BF16),
            pltpu.VMEM((ROWS, D), BF16),
            pltpu.VMEM((4, 2, ALL, 128), F32),
            pltpu.VMEM((4, ALL, 128), F32),
            pltpu.VMEM((24, 128), jnp.int32),
            pltpu.VMEM((768, 128), F32),
            pltpu.VMEM((ROWS, 128), F32),
            pltpu.VMEM((ROWS, 128), F32),
            pltpu.VMEM((192, 96), BF16),
            pltpu.VMEM((48, 192), BF16),
            pltpu.VMEM((4, 48, 128), BF16),
            pltpu.VMEM((4, 48, 128), BF16),
            pltpu.VMEM((4, 48, 128), BF16),
            pltpu.VMEM((8, 48, 128), BF16),
            pltpu.VMEM((12, 128), F32),
            pltpu.VMEM((12, 128), F32),
            pltpu.VMEM((TAPS, D), F32),
            pltpu.VMEM((12, 128), F32),
            pltpu.VMEM((12, 128), F32),
            pltpu.SemaphoreType.DMA((20,)),
            pltpu.SemaphoreType.DMA((4,)),
            pltpu.SemaphoreType.DMA((8,)),
            pltpu.SemaphoreType.DMA((SEMS,)),
            pltpu.SemaphoreType.DMA((SEMS,)),
        ],
        compiler_params=pltpu.CompilerParams(
            collective_id=0, has_side_effects=True, vmem_limit_bytes=60 << 20
        ),
        name="conformer",
    )(
        frames,
        segments.reshape(1024, 128),
        norm_gain.reshape(12, 128),
        norm_bias.reshape(12, 128),
        expand_weight,
        conv_kernel,
        batch_scale.reshape(12, 128),
        batch_shift.reshape(12, 128),
        project_weight.T,
    )


def solution(mesh):
    in_specs = (
        P(("dp", "fsdp"), None),
        P(),
        P(),
        P(),
        P("fsdp", "dp"),
        P(),
        P(),
        P(),
        P("fsdp", "dp"),
    )
    out_specs = P(("dp", "fsdp"), None)
    return jax.shard_map(local, mesh=mesh, in_specs=in_specs, out_specs=out_specs, check_vma=False)
```

```python
import functools

import jax
import jax.numpy as jnp
from jax import lax
from jax.experimental import pallas as pl
from jax.experimental.pallas import tpu as pltpu
from jax.sharding import PartitionSpec as P

EPSILON = 1e-05
MESH = pl.DeviceIdType.MESH
F32 = jnp.float32
BF16 = jnp.bfloat16

NX, NY, NZ = 4, 4, 8
ROWS = 512
EDGE = 16
ALL = ROWS + 2 * EDGE
D = 1536
HALF = 15
TAPS = 31
SEMS = 256


def sigmoid(v):
    return 0.5 * jnp.tanh(0.5 * v) + 0.5


def kernel(
    frames, segs, gain, bias, w1, taps, scale, shift, w2, out,
    wide, late, rows, normed, active, result, wider, gated, seg_raw, seg_col, before, after,
    own1, own2, pack1, pack2, parts1, parts2, gain_v, bias_v, taps_v, scale_v, shift_v,
    local_sem, part_send, part_recv, send_sem, recv_sem,
):
    dp = lax.axis_index("dp")
    z = lax.axis_index("fsdp")
    x = dp // 8
    y = (dp // 2) % 4
    c = dp % 2
    s = 1 - 2 * c
    block = dp * 8 + z

    def dev(px, py, pz, pc):
        return (px * 8 + py * 2 + pc, pz)

    def xo(k):
        return (x + k + 2 * NX) % NX

    def yo(k):
        return (y + k + 2 * NY) % NY

    def zo(k):
        return (z + k + 2 * NZ) % NZ

    nxt = (block + 1) % 256
    prv = (block + 255) % 256
    next_dev = (nxt // 8, nxt % 8)
    prev_dev = (prv // 8, prv % 8)

    u = jnp.where(c == 0, x, y)
    v = jnp.where(c == 0, y, x)

    def m4(k):
        return (k + 8) % 4

    def uv_dev(pu, pv):
        return dev(jnp.where(c == 0, pu, pv), jnp.where(c == 0, pv, pu), z, c)

    tile0 = block // 2
    seg_tiles = [
        jnp.maximum(tile0 - 1, 0),
        tile0,
        jnp.minimum(tile0 + 1, 127),
    ]
    loads = [
        pltpu.make_async_copy(w1, own1, local_sem.at[0]),
        pltpu.make_async_copy(w2, own2, local_sem.at[1]),
        pltpu.make_async_copy(frames, rows.at[pl.ds(EDGE, ROWS)], local_sem.at[2]),
        pltpu.make_async_copy(gain, gain_v, local_sem.at[3]),
        pltpu.make_async_copy(bias, bias_v, local_sem.at[4]),
        pltpu.make_async_copy(taps, taps_v, local_sem.at[5]),
        pltpu.make_async_copy(scale, scale_v, local_sem.at[6]),
        pltpu.make_async_copy(shift, shift_v, local_sem.at[7]),
    ] + [
        pltpu.make_async_copy(
            segs.at[pl.ds(pl.multiple_of(t * 8, 8), 8)],
            seg_raw.at[pl.ds(8 * i, 8)],
            local_sem.at[8 + i],
        )
        for i, t in enumerate(seg_tiles)
    ]
    for load in loads:
        load.start()

    barrier = pltpu.get_barrier_semaphore()
    peers = [
        dev(x, yo(dy), z, (c + dc) % 2) for dy in range(NY) for dc in range(2) if dy + dc
    ]
    peers += [dev(x, y, zo(k), c) for k in range(1, NZ)]
    peers += [dev(xo(k), y, z, c) for k in range(1, NX)]
    peers += [next_dev, prev_dev]
    for peer in peers:
        pl.semaphore_signal(barrier, inc=1, device_id=peer, device_id_type=MESH)
    pl.semaphore_wait(barrier, len(peers))

    count = [0]
    sent = []

    class Copy:
        def __init__(self, src, dst, device, when=None, heard=None):
            self.src, self.dst, self.device, self.when, self.heard = src, dst, device, when, heard
            self.i = count[0]
            count[0] += 1
            sent.append(self)
            self._on(when, "start")

        def _on(self, when, method):
            def act():
                copy = pltpu.make_async_remote_copy(
                    src_ref=self.src(), dst_ref=self.dst(), send_sem=send_sem.at[self.i],
                    recv_sem=recv_sem.at[self.i], device_id=self.device(), device_id_type=MESH,
                )
                getattr(copy, method)()

            if when is None:
                act()
            else:
                pl.when(c == when)(act)

        def wait_recv(self):
            self._on(self.heard, "wait_recv")

        def wait_send(self):
            self._on(self.when, "wait_send")

    def drain():
        while sent:
            sent.pop(0).wait_send()

    def send(ref, device, when=None, heard=None):
        return Copy(ref, ref, device, when, heard)

    def to_sibling():
        return dev(x, y, z, 1 - c)

    def mirror(ref, when=None, heard=None):
        return send(ref, to_sibling, when, heard)

    hz = (pl.ds(0, 4), pl.ds(4, 4))
    whole = slice(None)
    rest = pl.ds(1, 2)
    order = (0, -1, 1, 2)
    st = {}

    def hx():
        return pl.ds(pl.multiple_of(2 * c, 2), 2)

    def wait(key):
        for copy in st[key]:
            copy.wait_recv()

    def line(p, du, i, zz=whole):
        return lambda: wide.at[c, p, m4(u + du), zz, m4(v + order[i])]

    def u_to(k):
        return lambda: uv_dev(m4(u + k), v)

    def v_to(k):
        return lambda: uv_dev(u, m4(v + k))

    def plane(p, du):
        return lambda: wide.at[c, p, m4(u + du)]

    def z_direct(p, key):
        st[key] = [
            send(lambda: wide.at[c, p, u, z, v], lambda k=k: dev(x, y, zo(k), c))
            for k in (4, 3, -3, 2, -2, 1, -1)
        ]

    def u_line(p, i):
        st.setdefault(("um", p), []).append(send(line(p, 0, i), u_to(1)))
        st.setdefault(("up", p), []).append(send(line(p, 0, i), u_to(-1)))

    def v_first():
        wait("z0")
        st["v0"] = [send(line(0, 0, 0), v_to(k)) for k in (1, -1, 2)]
        u_line(0, 0)
        z_direct(rest, "zr")

    def v_rest():
        wait("zr")
        st["vr"] = [send(line(rest, 0, 0), v_to(k)) for k in (1, -1)]

    def u_first(i):
        st["v0"][i - 1].wait_recv()
        u_line(0, i)
        if i == 3:
            st["m", 0] = [mirror(plane(0, 0))]

    def v_relay():
        st["vr"][0].wait_recv()
        a = send(line(rest, 0, 1, hz[0]), v_to(1))
        st["vr"][1].wait_recv()
        b = send(line(rest, 0, 2, hz[1]), v_to(-1))
        st["vr2"] = [a, b]

    def u_lines(p):
        for i in range(3):
            u_line(p, i)
        if p == 1:
            wait("vr2")
        u_line(p, 3)
        st["m", p] = [mirror(plane(p, 0))]

    def relay(p, i):
        halves = st.setdefault(("h", p), [])
        st["um", p][i].wait_recv()
        halves.append(send(line(p, -1, i, hz[0]), u_to(1)))
        st["up", p][i].wait_recv()
        halves.append(send(line(p, 1, i, hz[1]), u_to(-1)))
        if i == 3:
            st["m", p].append(mirror(plane(p, -1)))
            st["m", p].append(mirror(plane(p, 1)))

    def u_end(p):
        wait(("h", p))
        st["m", p].append(mirror(plane(p, 2)))

    def x_to():
        return dev(xo(s), y, z, c)

    def y_to():
        return dev(x, yo(s), z, c)

    def z_to():
        return dev(x, y, zo(s), c)

    def c_first():
        st["cx"] = send(lambda: late.at[:, x, z, y], x_to)
        st["cx2"] = send(lambda: late.at[:, x, z, y], lambda: dev(xo(2), y, z, c), 0, 0)

    def c_x():
        st["cx"].wait_recv()
        st["cmx"] = mirror(lambda: late.at[:, xo(-s), z, y])
        st["cx2"].wait_recv()
        st["cmx2"] = mirror(lambda: late.at[:, xo(2), z, y], 0, 1)

    def c_line(k, i, xx=None):
        return lambda: late.at[:, whole if xx is None else xx(), zo(-s * k), yo(s * order[i])]

    def c_y():
        st["cmx"].wait_recv()
        st["cmx2"].wait_recv()
        st["cy"] = send(c_line(0, 0), y_to)
        st["cz", 1] = [send(c_line(0, 0), z_to)]

    def c_y1():
        st["cy"].wait_recv()
        st["cy2"] = send(c_line(0, 1, hx), y_to)
        st["cmy"] = mirror(c_line(0, 1))
        st["cz", 1].append(send(c_line(0, 1), z_to))

    def c_y2():
        st["cmy"].wait_recv()
        st["cz", 1].append(send(c_line(0, 2), z_to))
        st["cy2"].wait_recv()
        st["cmy2"] = mirror(c_line(0, 3, hx))

    def c_y3():
        st["cmy2"].wait_recv()
        st["cz", 1].append(send(c_line(0, 3), z_to))

    def c_z(k, i):
        st["cz", k][i].wait_recv()
        if k < 4:
            part = hx if k == 3 else None
            st.setdefault(("cz", k + 1), []).append(send(c_line(k, i, part), z_to))
        if i == 3:
            if k < 4:
                st.setdefault("mc", []).append(mirror(lambda: late.at[:, :, zo(-s * k)]))
            else:
                st["mc"].append(mirror(lambda: late.at[:, hx(), zo(4)]))

    loads[0].wait()
    for k in range(4):
        pack1[k] = jnp.concatenate(
            [own1[48 * k : 48 * k + 48, :].astype(F32), jnp.zeros((48, 32), F32)], axis=1
        ).astype(BF16)
    home = y // 2
    slot = (y % 2) * 2 + c

    def part_copy(dy, core):
        return pltpu.make_async_remote_copy(
            src_ref=pack1.at[yo(dy)], dst_ref=parts1.at[slot], send_sem=part_send.at[dy],
            recv_sem=part_recv.at[2 * dy + core], device_id=dev(x, yo(dy), z, home), device_id_type=MESH,
        )

    for dy in (2, 1, 3):
        part_copy(dy, c).start()

    @pl.when(c == home)
    def _():
        parts1[slot] = pack1[y]

    @pl.when(c != home)
    def _():
        part_copy(0, c).start()

    loads[1].wait()
    own2r = jnp.transpose(own2[...].astype(F32))
    for k in range(4):
        pack2[k] = jnp.concatenate(
            [own2r[48 * k : 48 * k + 48, :], jnp.zeros((48, 80), F32)], axis=1
        ).astype(BF16)
    mine = y * 2 + c
    spread = []
    for dy, dc in ((2, 0), (2, 1), (1, 0), (3, 0), (1, 1), (3, 1), (0, 1)):
        spread.append(
            Copy(
                lambda dy=dy: pack2.at[yo(dy)],
                lambda: parts2.at[mine],
                lambda dy=dy, dc=dc: dev(x, yo(dy), z, (c + dc) % 2),
            )
        )
    parts2[mine] = pack2[y]

    for dy in range(4):
        for core in range(2):
            due = yo(-dy) // 2 == c
            if dy == 0:
                due = jnp.logical_and(due, c != core)

            @pl.when(due)
            def _(dy=dy, core=core):
                part_copy(dy, core).wait_recv()

    full1 = jnp.concatenate([parts1[i, :, :96].astype(F32) for i in range(4)], axis=1).astype(BF16)
    for p in range(3):
        wide[c, p, u, z, v] = full1[:, 128 * p : 128 * p + 128]
    z_direct(0, "z0")

    loads[2].wait()
    halo = [
        Copy(
            lambda: rows.at[pl.ds(EDGE, EDGE)], lambda: rows.at[pl.ds(EDGE + ROWS, EDGE)], lambda: prev_dev
        ),
        Copy(lambda: rows.at[pl.ds(ROWS, EDGE)], lambda: rows.at[pl.ds(0, EDGE)], lambda: next_dev),
    ]

    for copy in spread:
        copy.wait_recv()
    full2 = jnp.concatenate([parts2[i, :, :48].astype(F32) for i in range(8)], axis=1).astype(BF16)
    for p in range(3):
        late[p, x, z, y] = full2[:, 128 * p : 128 * p + 128]
    c_first()

    loads[3].wait()
    loads[4].wait()

    gain_row = jnp.concatenate([gain_v[i : i + 1, :] for i in range(12)], axis=1)
    bias_row = jnp.concatenate([bias_v[i : i + 1, :] for i in range(12)], axis=1)

    def norm(r0, n):
        v = rows[pl.ds(r0, n), :].astype(F32)
        mean = jnp.sum(v, axis=1, keepdims=True) * (1.0 / D)
        v = v - mean
        var = jnp.sum(v * v, axis=1, keepdims=True) * (1.0 / D)
        normed[pl.ds(r0, n), :] = (
            v * lax.rsqrt(var + EPSILON) * gain_row + bias_row
        ).astype(BF16)

    @pl.loop(0, 8)
    def _(i):
        norm(pl.multiple_of(EDGE + i * 32, 16), 32)

    v_first()
    c_x()
    c_y()

    @pl.loop(8, 16)
    def _(i):
        norm(pl.multiple_of(EDGE + i * 32, 16), 32)

    u_first(1)
    u_first(2)
    u_first(3)
    v_rest()
    c_y1()

    for copy in halo:
        copy.wait_recv()
    norm(0, EDGE)
    norm(EDGE + ROWS, EDGE)

    for load in loads[5:]:
        load.wait()
    base = (block * 4) % 8 + 8
    for i in range(6):
        q = base + i - 1
        there = block * 4 + i - 1
        row = seg_raw[pl.ds(q, 1), :].astype(F32)
        row = jnp.where(jnp.logical_or(there < 0, there >= 1024), -1.0, row)
        seg_col[pl.ds(128 * i, 128), :] = jnp.transpose(jnp.broadcast_to(row, (128, 128)))

    @pl.loop(0, 16)
    def _(i):
        r0 = pl.multiple_of(i * 32, 32)
        center = seg_col[pl.ds(r0 + 128, 32), :]
        low = jnp.zeros((32, 128), F32)
        high = jnp.zeros((32, 128), F32)
        for d in range(1, HALF + 1):
            low = low + jnp.where(seg_col[pl.ds(r0 + 128 - d, 32), :] == center, 1.0, 0.0)
            high = high + jnp.where(seg_col[pl.ds(r0 + 128 + d, 32), :] == center, 1.0, 0.0)
        before[pl.ds(r0, 32), :] = low
        after[pl.ds(r0, 32), :] = high

    v_relay()
    c_y2()
    relay(0, 0)
    relay(0, 1)
    c_y3()
    relay(0, 2)
    relay(0, 3)
    u_lines(1)
    c_z(1, 0)
    c_z(1, 1)
    u_end(0)
    relay(1, 0)
    c_z(1, 2)

    def operand(m, p, g):
        if m == 0:
            return wide[0, p, g].reshape(D, 128)
        return jnp.concatenate([wide[1, p, k % 4, k // 4, g] for k in range(32)], axis=0)

    def expand(p, j):
        rhs = jnp.concatenate([operand(m, p, 2 * j + h) for h in (0, 1) for m in (0, 1)], axis=1)
        both = jnp.dot(normed[...], rhs, preferred_element_type=F32)
        for h in (0, 1):
            for m in (0, 1):
                k = 128 * (2 * h + m)
                wider[2 * j + h, m] = both[:, k : k + 128]

    def gate():
        @pl.loop(0, ALL // 32)
        def _(i):
            r = pl.ds(pl.multiple_of(i * 32, 32), 32)
            for g in (0, 1):
                for m in (0, 1):
                    t = wider[g, m, r, :] * sigmoid(wider[g + 2, m, r, :])
                    gated[2 * g + m, r, :] = t.astype(BF16).astype(F32)

    def conv(p, i):
        tiles = [6 * g + 3 * m + p for g in range(2) for m in range(2)]
        r0 = pl.multiple_of(i * 32, 32)
        low = before[pl.ds(r0, 32), :]
        high = after[pl.ds(r0, 32), :]
        sums = [None] * 4
        for o in range(TAPS):
            d = o - HALF
            keep = low >= float(-d) if d < 0 else high >= float(d)
            for k, l in enumerate(tiles):
                t = gated[k, pl.ds(r0 + o + 1, 32), :]
                if d != 0:
                    t = jnp.where(keep, t, 0.0)
                t = t * taps_v[o : o + 1, 128 * l : 128 * l + 128]
                sums[k] = t if sums[k] is None else sums[k] + t
        for k, l in enumerate(tiles):
            h = sums[k] * scale_v[l : l + 1, :] + shift_v[l : l + 1, :]
            h = (h * sigmoid(h)).astype(BF16)
            active[pl.ds(r0, 32), 512 * p + 128 * k : 512 * p + 128 * k + 128] = h

    def project(k):
        starts = [128 * (6 * h + 3 * m + p) for p in range(3) for h in (0, 1) for m in (0, 1)]
        tiles = [late[i % 3, i // 3].reshape(D, 128) for i in range(4 * k, 4 * k + 4)]
        rhs = jnp.concatenate(
            [jnp.concatenate([t[a : a + 128] for a in starts], axis=0) for t in tiles], axis=1
        )
        return jnp.dot(active[...], rhs, preferred_element_type=F32)

    def quarters(body, slots, steps=4):
        if steps == 2:
            slots = [sum(slots[:2], []), sum(slots[2:], [])]

        @pl.loop(0, steps)
        def _(j):
            body(j)
            for k, events in enumerate(slots):
                if events:

                    @pl.when(j == k)
                    def _(events=events):
                        for event in events:
                            event()

    E = functools.partial

    def conv_alone(p):
        def body(j):
            for q in range(4):
                conv(p, 4 * j + q)

        return body

    def expand_alone(p):
        return lambda j: expand(p, j)

    for dy in (1, 2, 3):
        part_copy(dy, c).wait_send()

    @pl.when(c != home)
    def _():
        part_copy(0, c).wait_send()

    wait(("m", 0))
    quarters(
        expand_alone(0), [[E(relay, 1, 1)], [E(c_z, 1, 3)], [E(relay, 1, 2)], [E(relay, 1, 3), E(u_lines, 2)]], 2
    )
    gate()
    quarters(
        conv_alone(0),
        [[E(c_z, 2, 0)], [E(c_z, 2, 1)], [E(u_end, 1), E(relay, 2, 0)], [E(c_z, 2, 2), E(relay, 2, 1)]],
    )
    wait(("m", 1))
    quarters(
        expand_alone(1), [[E(c_z, 2, 3)], [E(relay, 2, 2)], [E(c_z, 3, 0)], [E(relay, 2, 3), E(c_z, 3, 1)]], 2
    )
    gate()
    quarters(conv_alone(1), [[E(c_z, 3, 2)], [E(u_end, 2)], [E(c_z, 3, 3)], [E(c_z, 4, 0)]])
    wait(("m", 2))
    quarters(expand_alone(2), [[], [E(c_z, 4, 1)], [], [E(c_z, 4, 2)]], 2)
    gate()
    quarters(conv_alone(2), [[E(c_z, 4, 3)], [], [], []])
    wait("mc")
    stores = []
    for g in range(3):
        cols = pl.ds(512 * g, 512)
        product = project(g)
        result[:, cols] = (product + rows[pl.ds(EDGE, ROWS), cols].astype(F32)).astype(BF16)
        store = pltpu.make_async_copy(result.at[:, cols], out.at[:, cols], local_sem.at[13 + g])
        store.start()
        stores.append(store)
    drain()
    for store in stores:
        store.wait()


def local(frames, segments, norm_gain, norm_bias, expand_weight, conv_kernel, batch_scale, batch_shift, project_weight):
    return pl.pallas_call(
        kernel,
        out_shape=jax.ShapeDtypeStruct((ROWS, D), BF16),
        in_specs=[pl.BlockSpec(memory_space=pltpu.HBM)] * 9,
        out_specs=pl.BlockSpec(memory_space=pltpu.HBM),
        scratch_shapes=[
            pltpu.VMEM((2, 3, 4, NZ, 4, 48, 128), BF16),
            pltpu.VMEM((3, NX, NZ, NY, 48, 128), BF16),
            pltpu.VMEM((ALL, D), BF16),
            pltpu.VMEM((ALL, D), BF16),
            pltpu.VMEM((ROWS, D), BF16),
            pltpu.VMEM((ROWS, D), BF16),
            pltpu.VMEM((4, 2, ALL, 128), F32),
            pltpu.VMEM((4, ALL, 128), F32),
            pltpu.VMEM((24, 128), jnp.int32),
            pltpu.VMEM((768, 128), F32),
            pltpu.VMEM((ROWS, 128), F32),
            pltpu.VMEM((ROWS, 128), F32),
            pltpu.VMEM((192, 96), BF16),
            pltpu.VMEM((48, 192), BF16),
            pltpu.VMEM((4, 48, 128), BF16),
            pltpu.VMEM((4, 48, 128), BF16),
            pltpu.VMEM((4, 48, 128), BF16),
            pltpu.VMEM((8, 48, 128), BF16),
            pltpu.VMEM((12, 128), F32),
            pltpu.VMEM((12, 128), F32),
            pltpu.VMEM((TAPS, D), F32),
            pltpu.VMEM((12, 128), F32),
            pltpu.VMEM((12, 128), F32),
            pltpu.SemaphoreType.DMA((20,)),
            pltpu.SemaphoreType.DMA((4,)),
            pltpu.SemaphoreType.DMA((8,)),
            pltpu.SemaphoreType.DMA((SEMS,)),
            pltpu.SemaphoreType.DMA((SEMS,)),
        ],
        compiler_params=pltpu.CompilerParams(
            collective_id=0, has_side_effects=True, vmem_limit_bytes=60 << 20
        ),
        name="conformer",
    )(
        frames,
        segments.reshape(1024, 128),
        norm_gain.reshape(12, 128),
        norm_bias.reshape(12, 128),
        expand_weight,
        conv_kernel,
        batch_scale.reshape(12, 128),
        batch_shift.reshape(12, 128),
        project_weight.T,
    )


def solution(mesh):
    in_specs = (
        P(("dp", "fsdp"), None),
        P(),
        P(),
        P(),
        P("fsdp", "dp"),
        P(),
        P(),
        P(),
        P("fsdp", "dp"),
    )
    out_specs = P(("dp", "fsdp"), None)
    return jax.shard_map(local, mesh=mesh, in_specs=in_specs, out_specs=out_specs, check_vma=False)
```
